32 devices in a mesh: section: 4 (over y, x), fsdp: 8 (over z, core).
Axes of the slice: x: 2, y: 2, z: 4, core: 2. Of those that a mesh axis runs over, the one named last changes fastest.
Arguments:
- inputs: bfloat16 [3, 32, 3072], P(None, 'fsdp'), may hold values from -6 to 6
- gain: float32 [4, 3072], P('section'), may hold values from 0.25 to 1.75
- w_gate: bfloat16 [4, 4, 3072, 8192], P('section', None, None, 'fsdp'), may hold values from -0.109375 to 0.109375
- w_up: bfloat16 [4, 4, 3072, 8192], P('section', None, None, 'fsdp'), may hold values from -0.109375 to 0.109375
- w_down: bfloat16 [4, 4, 8192, 3072], P('section', None, 'fsdp'), may hold values from -0.0625 to 0.0625
- routes: int32 [4, 3, 32, 2], P('section'), may hold values from 0 to 3, all different within a row
- shares: float32 [4, 3, 32, 2], P('section'), may hold values from 0.1 to 1
Outputs:
- hidden: bfloat16 [4, 3, 32, 3072], P('section', None, 'fsdp')
The draws below stay inside these ranges and needn't reach their ends.
Inputs may be any that keep to these rules, and one draw needn't show every extreme that they name: `routes`: each token names 2 different experts, and every expert is named in each microbatch of each layer.
All inputs are finite; a program needn't handle non-finite values.
Results may differ from the reference program's by a relative error of at most 0.014.
Values may be sent and summed in bfloat16 or wider, within the bound.
No kernel may reach another device: no remote copies, remote signals or barrier semaphores. Data moves between devices by JAX's collectives and lax.ppermute only.
A program may use at most 128 MiB of HBM per device.

```python
import math
import jax
import jax.numpy as jnp
from jax import lax

D = 3072
FF = 8192
E = 4
TOP = 2
BLOCK = 128
MICRO = 3
LAYERS = 4
TOKENS = 32


def block_scale(stream_key, extent, cuts, smallest, high):
    def one(dim, blocks):
        draws = jax.random.uniform(jax.random.fold_in(jax.random.fold_in(stream_key, 6), dim), (blocks,), jnp.float32, smallest / len(cuts), high / len(cuts))
        return jnp.repeat(jnp.exp(draws), extent[dim] // blocks).reshape((-1,) + (1,) * (len(extent) - dim - 1))

    loudness = one(*cuts[0])
    for cut in cuts[1:]:
        loudness = loudness * one(*cut)
    return loudness


def distinct(key, rows, number_of, top, lift):
    sequence = jax.random.permutation(jax.random.fold_in(key, 1), number_of)
    favour = sequence
    for power in range(3):
        favour = favour * favour // number_of
    favour = favour * lift // number_of
    chance = jax.random.randint(jax.random.fold_in(key, 2), (rows, number_of), 0, 4096) + favour
    fixed_rows = jax.random.permutation(jax.random.fold_in(key, 3), rows)[jnp.arange(number_of) % rows]
    chance = jnp.where(jnp.arange(rows)[:, None] == fixed_rows[None, :], 1 << 14, chance)
    priority = chance * number_of + jnp.arange(number_of)
    return lax.top_k(priority.astype(jnp.int32), top)[1].astype(jnp.int32)


def gaussian(rng, extent, deviation, limit, pieces=(), kind=jnp.bfloat16):
    array = jax.random.normal(rng, extent, jnp.float32) * deviation
    if len(pieces) > 0:
        array = block_scale(rng, extent, pieces, -0.22, 0.18) * array
    return jnp.clip(array, min=-limit, max=limit).astype(kind)


def setup_inputs(seed: int = 0) -> dict:
    streams_of = jax.random.split(jax.random.key(seed), 8)
    inputs = gaussian(streams_of[0], (MICRO, TOKENS, D), 1.0, 6.0, ((1, 8),))
    gain = jnp.clip(1.0 + 0.15 * jax.random.normal(streams_of[1], (LAYERS, D), jnp.float32), 0.25, 1.75)
    w_gate = gaussian(streams_of[2], (LAYERS, E, D, FF), D ** -0.5, 0.109375, ((0, 4), (3, 8)))
    w_up = gaussian(streams_of[3], (LAYERS, E, D, FF), D ** -0.5, 0.109375, ((0, 4), (3, 8)))
    w_down = gaussian(streams_of[4], (LAYERS, E, FF, D), FF ** -0.5, 0.0625, ((0, 4), (2, 8)))
    routes = distinct(streams_of[5], LAYERS * MICRO * TOKENS, E, TOP, 8192).reshape((LAYERS, MICRO, TOKENS, TOP))
    shares = jnp.clip(jnp.exp(math.log(1.0) - 2.3025851 * jax.random.uniform(streams_of[6], (LAYERS, MICRO, TOKENS, TOP), jnp.float32) ** block_scale(streams_of[6], (LAYERS, MICRO, TOKENS, TOP), ((0, 4),), -0.2, 0.2)), 0.1, 1.0)
    return {"inputs": inputs, "gain": gain, "w_gate": w_gate, "w_up": w_up, "w_down": w_down, "routes": routes, "shares": shares}


def arrange(choices, experts, block, nblocks):
    flat_choice = choices.reshape(-1).astype(jnp.int32)
    slots_used = flat_choice.shape[0]
    onehot = (flat_choice[:, None] == jnp.arange(experts, dtype=jnp.int32)[None, :]).astype(jnp.int32)
    counts = lax.optimization_barrier(jnp.sum(onehot, axis=0))
    padded = (counts + block - 1) // block * block
    ends = jnp.cumsum(padded).astype(jnp.int32)
    starts = ends - padded
    before = jnp.cumsum(onehot, axis=0) - onehot
    destination = lax.optimization_barrier(jnp.sum((before + starts[None, :]) * onehot, axis=1)).astype(jnp.int32)
    source = jnp.zeros((nblocks * block,), jnp.int32).at[destination].set(jnp.arange(slots_used, dtype=jnp.int32))
    slot_live = jnp.zeros((nblocks * block,), jnp.int32).at[destination].set(1)
    block_first = jnp.arange(nblocks, dtype=jnp.int32) * block
    block_expert = jnp.minimum(lax.optimization_barrier(jnp.sum((block_first[:, None] >= ends[None, :]).astype(jnp.int32), axis=1)), experts - 1).astype(jnp.int32)
    block_live = block_first < ends[experts - 1]
    return (destination, source, slot_live, block_expert, block_live)

def expert_mix(normed, choices, weights_share, gate_w, up_w, down_w):
    tokens, width = normed.shape
    experts = gate_w.shape[0]
    nblocks = (2 * tokens + BLOCK - 1) // BLOCK + experts
    destination, source, slot_live, block_expert, block_live = arrange(choices, experts, BLOCK, nblocks)
    picked_rows = jnp.where(slot_live[:, None] > 0, normed[source // 2], jnp.zeros((), normed.dtype))
    blocks = picked_rows.reshape(nblocks, BLOCK, width)

    def one_block(item):
        rows_block, expert_id, live = item

        def compute(operand):
            gate = jnp.dot(operand, gate_w[expert_id], preferred_element_type=jnp.float32)
            upward = jnp.dot(operand, up_w[expert_id], preferred_element_type=jnp.float32)
            gated = (jax.nn.silu(gate) * upward).astype(jnp.bfloat16)
            return jnp.dot(gated, down_w[expert_id], preferred_element_type=jnp.float32)

        def nothing(operand):
            return jnp.zeros((operand.shape[0], down_w.shape[2]), jnp.float32)
        return lax.cond(live, compute, nothing, rows_block)
    results = lax.map(one_block, (blocks, block_expert, block_live))
    results = results.reshape(nblocks * BLOCK, width)
    chosen = results[destination].reshape(tokens, 2, width)
    return lax.optimization_barrier(jnp.sum(chosen * weights_share[:, :, None].astype(jnp.float32), axis=1))

def rms_norm(rows, gain_row):
    values = rows.astype(jnp.float32)
    scale = lax.rsqrt(lax.optimization_barrier(jnp.mean(values * values, axis=-1, keepdims=True)) + 1e-05)
    return (values * scale * gain_row[None, :]).astype(jnp.bfloat16)

def reference(inputs, gain, w_gate, w_up, w_down, routes, shares):

    def layer(state, params):
        gain_row, gate_w, up_w, down_w, route_layer, share_layer = params

        def one_micro(item):
            rows, route_micro, share_micro = item
            normed = rms_norm(rows, gain_row)
            mixed = expert_mix(normed, route_micro, share_micro, gate_w, up_w, down_w)
            return (rows.astype(jnp.float32) + mixed).astype(jnp.bfloat16)
        result = lax.map(one_micro, (state, route_layer, share_layer))
        return (result, result)
    _, outputs = lax.scan(layer, inputs, (gain, w_gate, w_up, w_down, routes, shares))
    return outputs
```

```python
import functools

import jax
import jax.numpy as jnp
from jax import lax
from jax.experimental import pallas as pl
from jax.experimental.pallas import tpu as pltpu
from jax.sharding import PartitionSpec as P

F32 = jnp.float32
BF16 = jnp.bfloat16
MESH_AXES = ("section", "fsdp")
RESIDENT_BYTES = 36 * 2**20
SLOT_ROWS = 16
DOWN_SLOTS = 4
GATE_SLOTS = 2
VMEM = pl.BlockSpec(memory_space=pltpu.VMEM)
HBM = pl.BlockSpec(memory_space=pl.ANY)


def round_up(value, to):
    return (value + to - 1) // to * to


def moved(array, sections, places, target):
    pairs = []
    for section in range(sections):
        for place in range(places):
            for half in range(2):
                to_section, to_place, to_half = target(section, place, half)
                pairs.append(
                    (
                        (section * places + place) * 2 + half,
                        (to_section * places + to_place) * 2 + to_half,
                    )
                )
    return lax.ppermute(array, MESH_AXES, pairs)


def ring_of(tick, sections, half):
    others = [s for s in range(sections) if s not in (tick, tick + 1)]
    helper = others[half % len(others)]
    return [tick, helper, tick + 1] + [s for s in others if s != helper]


def after(tick, sections, half, section):
    ring = ring_of(tick, sections, half)
    return ring[(ring.index(section) + 1) % sections]


def position():
    index = lax.axis_index("fsdp")
    return index // 2, index % 2


def chained(kernel, outs, ins, held, specs=None, scratch=(), limit=24, flops=0, moved_bytes=0):
    specs = [VMEM] * len(ins) if specs is None else specs
    result = pl.pallas_call(
        kernel,
        out_shape=tuple(outs) + (pltpu.VMEM(held.shape, held.dtype),),
        in_specs=list(specs) + [VMEM],
        out_specs=(VMEM,) * (len(outs) + 1),
        input_output_aliases={len(ins): len(outs)},
        scratch_shapes=list(scratch),
        compiler_params=pltpu.CompilerParams(vmem_limit_bytes=limit * 2**20),
        cost_estimate=pl.CostEstimate(
            flops=flops, bytes_accessed=moved_bytes, transcendentals=0
        ),
    )(*ins, held)
    return result


def hold_kernel(resident, gate_ref, up_ref, comb_ref, held_ref, sems):
    copies = []
    for expert in range(resident):
        for which, ref in ((0, gate_ref), (1, up_ref)):
            slot = which * resident + expert
            copies.append(
                pltpu.make_async_copy(ref.at[0, expert], held_ref.at[slot], sems.at[slot])
            )
    for copy in copies:
        copy.start()
    for copy in copies:
        copy.wait()


def hold(w_gate, w_up, comb, resident):
    _, _, width, hidden = w_gate.shape
    shape = (2 * resident, width, hidden)
    return pl.pallas_call(
        functools.partial(hold_kernel, resident),
        out_shape=pltpu.VMEM(shape, BF16),
        in_specs=[HBM, HBM, HBM],
        out_specs=VMEM,
        scratch_shapes=[pltpu.SemaphoreType.DMA((2 * resident,))],
        compiler_params=pltpu.CompilerParams(vmem_limit_bytes=24 * 2**20),
        cost_estimate=pl.CostEstimate(
            flops=0, bytes_accessed=2 * 2 * resident * width * hidden, transcendentals=0
        ),
    )(w_gate, w_up, comb)


def picker(place, rows, local):
    row = lax.broadcasted_iota(jnp.int32, (SLOT_ROWS, rows), 0)
    column = lax.broadcasted_iota(jnp.int32, (SLOT_ROWS, rows), 1)
    return jnp.logical_and(row < local, column == place * local + row).astype(BF16)


def entry_kernel(places, local, *refs):
    chunks, out_ref = refs[:places], refs[places + 1]
    place, _ = position()
    rows = out_ref.shape[0]
    total = None
    for k in range(places):
        pick = picker(place ^ k, rows, local)
        part = lax.dot_general(
            pick, chunks[k][...], (((0,), (0,)), ((), ())), preferred_element_type=F32
        )
        total = part if total is None else total + part
    out_ref[...] = total.astype(BF16)


def block_at(ref, place, rows, columns, across):
    if across * columns == ref.shape[1] and rows == ref.shape[0]:
        row_start = 0
    else:
        row_start = pl.multiple_of(place // across * rows, 16)
    column_start = pl.multiple_of(place % across * columns, 128)
    return (pl.ds(row_start, rows), pl.ds(column_start, columns))


def split_kernel(places, across, keep_ref, got_ref, rows_ref, held_ref, *outs):
    place, _ = position()
    for k in range(places):
        out = outs[k]
        at = block_at(keep_ref, place ^ k, out.shape[0], out.shape[1], across)
        total = keep_ref[at] + got_ref[at].astype(F32)
        if k == 0:
            total = total + rows_ref[at].astype(F32)
        out[...] = total.astype(BF16)


def add_kernel(places, *refs):
    total = refs[0][...].astype(F32)
    for k in range(1, places):
        total = total + refs[k][...].astype(F32)
    refs[places + 1][...] = total.astype(BF16)


def join_kernel(places, across, local, tick, *refs):
    chunks, own_ref, out_ref, new_own_ref = (
        refs[:places], refs[places], refs[places + 2], refs[places + 3],
    )
    place, _ = position()
    for k in range(places):
        chunk = chunks[k]
        at = block_at(out_ref, place ^ k, chunk.shape[0], chunk.shape[1], across)
        out_ref[at] = chunk[...]

    active = lax.axis_index("section") == tick

    @pl.when(active)
    def _():
        pick = picker(place, out_ref.shape[0], local)
        new_own_ref[...] = jnp.dot(
            pick, out_ref[...], preferred_element_type=F32
        ).astype(BF16)

    @pl.when(jnp.logical_not(active))
    def _():
        new_own_ref[...] = own_ref[...]


def layer_kernel(tick, resident, half_rows, mine_ref, other_ref, gain_ref, comb_ref, gate_ref, up_ref,
                 down_ref, held_ref, keep_ref, send_ref, held_out, normed, part, gate_slots, down_slots,
                 gate_sems, down_sems):
    experts = gate_ref.shape[1]
    hidden = gate_ref.shape[3]
    piece = hidden // 2
    rows = mine_ref.shape[0]

    @pl.when(lax.axis_index("section") == tick)
    def _():
        queue = []
        for e in range(resident):
            queue += [("down", e, 0), ("down", e, 1)]
        for e in range(resident, experts):
            queue += [("gate", e, 0), ("up", e, 0), ("down", e, 0), ("down", e, 1),
                      ("gate", e, 1), ("up", e, 1)]
        numbers, counts = {}, {"down": 0, "gate": 0}
        for kind, e, s in queue:
            pool = "down" if kind == "down" else "gate"
            numbers[kind, e, s] = (pool, counts[pool])
            counts[pool] += 1
        slots = {"down": DOWN_SLOTS, "gate": GATE_SLOTS}
        freed = {"down": 0, "gate": 0}
        pending = list(queue)

        def copy_of(item):
            kind, e, s = item
            pool, number = numbers[item]
            slot = number % slots[pool]
            cut = pl.ds(s * piece, piece)
            if kind == "down":
                return pltpu.make_async_copy(
                    down_ref.at[0, e, cut, :], down_slots.at[slot], down_sems.at[slot]
                ), down_slots.at[slot]
            source = gate_ref if kind == "gate" else up_ref
            return pltpu.make_async_copy(
                source.at[0, e, :, cut], gate_slots.at[slot], gate_sems.at[slot]
            ), gate_slots.at[slot]

        def issue():
            while pending:
                pool, number = numbers[pending[0]]
                if number >= freed[pool] + slots[pool]:
                    return
                copy_of(pending.pop(0))[0].start()

        def times(left, item):
            copy, ref = copy_of(item)
            copy.wait()
            result = jnp.dot(left, ref[...], preferred_element_type=F32)
            return result

        def done(item):
            freed[numbers[item][0]] += 1
            issue()

        issue()
        for ref, start in ((mine_ref, 0), (other_ref, half_rows)):
            values = ref[...].astype(F32)
            scale = lax.rsqrt(jnp.mean(values * values, axis=-1, keepdims=True) + 1e-05)
            normed[start:start + rows, :] = (values * scale * gain_ref[...]).astype(BF16)
            if half_rows > rows:
                normed[start + rows:start + half_rows, :] = jnp.zeros(
                    (half_rows - rows, values.shape[1]), BF16
                )

        def activated(gate, up, e):
            return (gate / (1.0 + jnp.exp(-gate)) * up * comb_ref[:, e:e + 1]).astype(BF16)

        first = True
        for e in range(experts):
            if e < resident:
                gate = jnp.dot(normed[...], held_ref[e], preferred_element_type=F32)
                up = jnp.dot(normed[...], held_ref[resident + e], preferred_element_type=F32)
                gated = activated(gate, up, e)
            for s in range(2):
                if e < resident:
                    left = gated[:, s * piece:(s + 1) * piece]
                else:
                    gate = times(normed[...], ("gate", e, s))
                    done(("gate", e, s))
                    up = times(normed[...], ("up", e, s))
                    done(("up", e, s))
                    left = activated(gate, up, e)
                if first:
                    part[...] = times(left, ("down", e, s))
                else:
                    part[...] += times(left, ("down", e, s))
                first = False
                done(("down", e, s))
        keep_ref[...] = part[0:rows, :]
        send_ref[...] = part[half_rows:half_rows + rows, :].astype(BF16)


def split_rows_kernel(places, local, keep_ref, got_ref, rows_ref, held_ref, *outs):
    place, _ = position()
    rows = keep_ref.shape[0]
    total = (keep_ref[...] + got_ref[...].astype(F32)).astype(BF16)
    for k in range(1, places):
        outs[k][...] = jnp.dot(
            picker(place ^ k, rows, local), total, preferred_element_type=F32
        ).astype(BF16)
    pick = picker(place, rows, local)
    outs[0][...] = jnp.dot(pick, total, preferred_element_type=F32) + jnp.dot(
        pick, rows_ref[...], preferred_element_type=F32
    )


def last_kernel(places, *refs):
    own_ref, chunks, before_ref, out_ref = refs[0], refs[1:places], refs[places], refs[places + 1]
    total = own_ref[...]
    for chunk in chunks:
        total = total + chunk[...].astype(F32)
    last = lax.axis_index("section") == lax.axis_size("section") - 1
    result = jnp.where(last, total, before_ref[...].astype(F32)).astype(BF16)
    micro, local_rows, _ = out_ref.shape
    for m in range(micro):
        out_ref[m] = result[m * local_rows:(m + 1) * local_rows, :]


def on_device(inputs, gain, w_gate, w_up, w_down, routes, shares):
    sections = lax.axis_size("section")
    places = lax.axis_size("fsdp") // 2
    micro, local_rows, width = inputs.shape
    _, experts, _, hidden = w_gate.shape
    local = micro * local_rows
    rows = places * local
    half_rows = round_up(rows, 64)
    across = places
    while (width // across) % 128 or width % across:
        across //= 2
    block = (rows // (places // across), width // across)
    resident = min(experts, RESIDENT_BYTES // (4 * width * hidden))
    half = lax.axis_index("fsdp") % 2

    def by_half(array):
        cut = array[0].reshape(micro, places, 2, local_rows, -1)
        return cut.transpose(2, 1, 0, 3, 4).reshape(2, rows, -1)

    chosen = by_half(routes)[..., None] == jnp.arange(experts, dtype=jnp.int32)
    comb = jnp.sum(jnp.where(chosen, by_half(shares)[..., None], 0.0), axis=2)
    comb = jnp.where(half == 0, comb, comb[::-1])
    comb = jnp.pad(comb, ((0, 0), (0, half_rows - rows), (0, 0))).reshape(2 * half_rows, experts)

    def swapped(array):
        return moved(array, sections, places, lambda s, p, c: (s, p, 1 - c))

    def within(array, k):
        return moved(array, sections, places, lambda s, p, c: (s, p ^ k, c))

    def onward(array, tick, k):
        return moved(
            array, sections, places, lambda s, p, c: (after(tick, sections, c, s), p ^ k, c)
        )

    def like(shape, dtype=BF16):
        return jax.ShapeDtypeStruct(shape, dtype)

    entry = jnp.pad(inputs.reshape(local, width), ((0, SLOT_ROWS - local), (0, 0)))
    pieces = [entry] + [within(entry, k) for k in range(1, places)]
    held = hold(w_gate, w_up, comb, resident)
    mine, held = chained(
        functools.partial(entry_kernel, places, local), [like((rows, width))], pieces, held
    )
    own = entry
    stream_flops = 6 * 2 * half_rows * width * hidden * experts
    stream_bytes = 2 * 3 * width * hidden * experts - 4 * width * hidden * resident
    for tick in range(sections):
        other = swapped(mine)
        keep, send, held = chained(
            functools.partial(layer_kernel, tick, resident, half_rows),
            [like((rows, width), F32), like((rows, width))],
            [mine, other, gain, comb, w_gate, w_up, w_down],
            held,
            specs=[VMEM, VMEM, VMEM, VMEM, HBM, HBM, HBM],
            scratch=[
                pltpu.VMEM((2 * half_rows, width), BF16),
                pltpu.VMEM((2 * half_rows, width), F32),
                pltpu.VMEM((GATE_SLOTS, width, hidden // 2), BF16),
                pltpu.VMEM((DOWN_SLOTS, hidden // 2, width), BF16),
                pltpu.SemaphoreType.DMA((GATE_SLOTS,)),
                pltpu.SemaphoreType.DMA((DOWN_SLOTS,)),
            ],
            limit=24,
            flops=stream_flops,
            moved_bytes=stream_bytes,
        )
        got = swapped(send)
        if tick + 1 == sections:
            break
        *blocks, held = chained(
            functools.partial(split_kernel, places, across),
            [like(block)] * places, [keep, got, mine], held,
        )
        blocks = [onward(blocks[k], tick, k) for k in range(places)]
        summed, held = chained(
            functools.partial(add_kernel, places), [like(block)], blocks, held
        )
        blocks = [onward(summed, tick, k) for k in range(places)]
        mine, own, held = chained(
            functools.partial(join_kernel, places, across, local, tick + 1),
            [like((rows, width)), like((SLOT_ROWS, width))], blocks + [own], held,
        )
    before = moved(own, sections, places, lambda s, p, c: ((s - 1) % sections, p, c))
    *pieces, held = chained(
        functools.partial(split_rows_kernel, places, local),
        [like((SLOT_ROWS, width), F32)] + [like((SLOT_ROWS, width))] * (places - 1),
        [keep, got, mine], held,
    )
    pieces = [pieces[0]] + [within(pieces[k], k) for k in range(1, places)]
    result = pl.pallas_call(
        functools.partial(last_kernel, places),
        out_shape=like((micro, local_rows, width)),
        in_specs=[VMEM] * (places + 1),
        out_specs=VMEM,
    )(*pieces, before)
    return result[None]


def solution(mesh):
    placed = (
        P(None, "fsdp", None),
        P("section", None),
        P("section", None, None, "fsdp"),
        P("section", None, None, "fsdp"),
        P("section", None, "fsdp", None),
        P("section", None, None, None),
        P("section", None, None, None),
    )
    return jax.shard_map(
        on_device,
        mesh=mesh,
        in_specs=placed,
        out_specs=P("section", None, "fsdp", None),
        check_vma=False,
    )
```

```python
import functools

import jax
import jax.numpy as jnp
from jax import lax
from jax.experimental import pallas as pl
from jax.experimental.pallas import tpu as pltpu
from jax.sharding import PartitionSpec as P

F32 = jnp.float32
BF16 = jnp.bfloat16
MESH_AXES = ("section", "fsdp")
RESIDENT_BYTES = 36 * 2**20
SCOPED_BYTES = 24 * 2**20
SLOT_ROWS = 16
DOWN_SLOTS = 4

GATE_SLOTS = 2
VMEM = pl.BlockSpec(memory_space=pltpu.VMEM)
HBM = pl.BlockSpec(memory_space=pl.ANY)


def round_up(value, to):
    return (value + to - 1) // to * to


def moved(array, sections, places, target):
    pairs = []
    for section in range(sections):
        for place in range(places):
            for half in range(2):
                goal = target(section, place, half)
                if goal is None:
                    continue
                to_section, to_place, to_half = goal
                pairs.append(
                    (
                        (section * places + place) * 2 + half,
                        (to_section * places + to_place) * 2 + to_half,
                    )
                )
    return lax.ppermute(array, MESH_AXES, pairs)


def ring_of(tick, sections, half):
    others = [s for s in range(sections) if s not in (tick, tick + 1)]
    helper = others[half % len(others)]
    return [tick, helper, tick + 1] + [s for s in others if s != helper]


def after(tick, sections, half, section):
    ring = ring_of(tick, sections, half)
    return ring[(ring.index(section) + 1) % sections]


def position():
    index = lax.axis_index("fsdp")
    return index // 2, index % 2


def chained(kernel, outs, ins, held, specs=None, scratch=(), pinned=99, flops=0,
            moved_bytes=0):
    specs = [VMEM] * len(ins) if specs is None else specs
    ins = [
        pltpu.with_memory_space_constraint(array, pltpu.VMEM)
        if spec is VMEM and i < pinned
        else array
        for i, (array, spec) in enumerate(zip(ins, specs, strict=True))
    ]
    result = pl.pallas_call(
        kernel,
        out_shape=tuple(
            pltpu.VMEM(out.shape, out.dtype) for out in (held, *outs)
        ),
        in_specs=[VMEM] + list(specs),
        out_specs=(VMEM,) * (len(outs) + 1),
        input_output_aliases={0: 0},
        scratch_shapes=list(scratch),
        compiler_params=pltpu.CompilerParams(vmem_limit_bytes=SCOPED_BYTES),
        cost_estimate=pl.CostEstimate(
            flops=flops, bytes_accessed=moved_bytes, transcendentals=0
        ),
    )(held, *ins)
    return result


def hold_kernel(resident, gate_ref, up_ref, comb_ref, held_ref, sems):
    copies = []
    for expert in range(resident):
        for which, ref in ((0, gate_ref), (1, up_ref)):
            slot = which * resident + expert
            copies.append(
                pltpu.make_async_copy(ref.at[0, expert], held_ref.at[slot], sems.at[slot])
            )
    for copy in copies:
        copy.start()
    for copy in copies:
        copy.wait()


def hold(w_gate, w_up, comb, resident):
    _, _, width, hidden = w_gate.shape
    shape = (2 * resident, width, hidden)
    return pl.pallas_call(
        functools.partial(hold_kernel, resident),
        out_shape=pltpu.VMEM(shape, BF16),
        in_specs=[HBM, HBM, HBM],
        out_specs=VMEM,
        scratch_shapes=[pltpu.SemaphoreType.DMA((2 * resident,))],
        compiler_params=pltpu.CompilerParams(vmem_limit_bytes=SCOPED_BYTES),
        cost_estimate=pl.CostEstimate(
            flops=0, bytes_accessed=2 * 2 * resident * width * hidden, transcendentals=0
        ),
    )(w_gate, w_up, comb)


def picker(place, rows, local):
    row = lax.broadcasted_iota(jnp.int32, (SLOT_ROWS, rows), 0)
    column = lax.broadcasted_iota(jnp.int32, (SLOT_ROWS, rows), 1)
    return jnp.logical_and(row < local, column == place * local + row).astype(BF16)


def entry_kernel(places, local, held_ref, *refs):
    chunks, out_ref = refs[:places], refs[places + 1]
    place, _ = position()
    rows = out_ref.shape[0]
    total = None
    for k in range(places):
        pick = picker(place ^ k, rows, local)
        part = lax.dot_general(
            pick, chunks[k][...], (((0,), (0,)), ((), ())), preferred_element_type=F32
        )
        total = part if total is None else total + part
    out_ref[...] = total.astype(BF16)


def block_at(ref, place, rows, columns, across):
    if across * columns == ref.shape[1] and rows == ref.shape[0]:
        row_start = 0
    else:
        row_start = pl.multiple_of(place // across * rows, 16)
    column_start = pl.multiple_of(place % across * columns, 128)
    return (pl.ds(row_start, rows), pl.ds(column_start, columns))


def split_kernel(places, across, held_ref, keep_ref, got_ref, rows_ref, held_out, *outs):
    place, _ = position()
    for k in range(places):
        out = outs[places - 1 - k]
        at = block_at(keep_ref, place ^ k, out.shape[0], out.shape[1], across)
        total = keep_ref[at] + got_ref[at].astype(F32)
        if k == 0:
            total = total + rows_ref[at].astype(F32)
        out[...] = total.astype(BF16)


def add_kernel(places, held_ref, *refs):
    total = refs[0][...].astype(F32)
    for k in range(1, places):
        total = total + refs[k][...].astype(F32)
    refs[places + 1][...] = total.astype(BF16)


def join_kernel(places, across, local, tick, held_ref, *refs):
    chunks, own_ref, out_ref, new_own_ref = (
        refs[:places], refs[places], refs[places + 2], refs[places + 3],
    )
    place, _ = position()
    for k in range(places):
        chunk = chunks[k]
        at = block_at(out_ref, place ^ k, chunk.shape[0], chunk.shape[1], across)
        out_ref[at] = chunk[...]

    active = lax.axis_index("section") == tick

    @pl.when(active)
    def _():
        pick = picker(place, out_ref.shape[0], local)
        new_own_ref[...] = jnp.dot(
            pick, out_ref[...], preferred_element_type=F32
        ).astype(BF16)

    @pl.when(jnp.logical_not(active))
    def _():
        new_own_ref[...] = own_ref[...]


def layer_kernel(tick, resident, half_rows, held_ref, mine_ref, other_ref, gain_ref, comb_ref, gate_ref,
                 up_ref, down_ref, held_out, keep_ref, send_ref, normed, part, gate_slots, down_slots,
                 gate_sems, down_sems):
    experts = gate_ref.shape[1]
    hidden = gate_ref.shape[3]
    piece = hidden // 2
    rows = mine_ref.shape[0]

    @pl.when(lax.axis_index("section") == tick)
    def _():
        queue = []
        for e in range(resident):
            queue += [("down", e, 0), ("down", e, 1)]
        for e in range(resident, experts):
            queue += [("gate", e, 0), ("up", e, 0), ("down", e, 0), ("down", e, 1),
                      ("gate", e, 1), ("up", e, 1)]
        numbers, counts = {}, {"down": 0, "gate": 0}
        for kind, e, s in queue:
            pool = "down" if kind == "down" else "gate"
            numbers[kind, e, s] = (pool, counts[pool])
            counts[pool] += 1
        slots = {"down": DOWN_SLOTS, "gate": GATE_SLOTS}
        freed = {"down": 0, "gate": 0}
        pending = list(queue)

        def copy_of(item):
            kind, e, s = item
            pool, number = numbers[item]
            slot = number % slots[pool]
            cut = pl.ds(s * piece, piece)
            if kind == "down":
                return pltpu.make_async_copy(
                    down_ref.at[0, e, cut, :], down_slots.at[slot], down_sems.at[slot]
                ), down_slots.at[slot]
            source = gate_ref if kind == "gate" else up_ref
            return pltpu.make_async_copy(
                source.at[0, e, :, cut], gate_slots.at[slot], gate_sems.at[slot]
            ), gate_slots.at[slot]

        def issue():
            while pending:
                pool, number = numbers[pending[0]]
                if number >= freed[pool] + slots[pool]:
                    return
                copy_of(pending.pop(0))[0].start()

        def times(left, item):
            copy, ref = copy_of(item)
            copy.wait()
            result = jnp.dot(left, ref[...], preferred_element_type=F32)
            return result

        def done(item):
            freed[numbers[item][0]] += 1
            issue()

        issue()
        for ref, start in ((mine_ref, 0), (other_ref, half_rows)):
            values = ref[...].astype(F32)
            scale = lax.rsqrt(jnp.mean(values * values, axis=-1, keepdims=True) + 1e-05)
            normed[start:start + rows, :] = (values * scale * gain_ref[...]).astype(BF16)
            if half_rows > rows:
                normed[start + rows:start + half_rows, :] = jnp.zeros(
                    (half_rows - rows, values.shape[1]), BF16
                )

        def activated(gate, up, e):
            return (gate / (1.0 + jnp.exp(-gate)) * up * comb_ref[:, e:e + 1]).astype(BF16)

        first = True
        for e in range(experts):
            if e < resident:
                gate = jnp.dot(normed[...], held_ref[e], preferred_element_type=F32)
                up = jnp.dot(normed[...], held_ref[resident + e], preferred_element_type=F32)
                gated = activated(gate, up, e)
            for s in range(2):
                if e < resident:
                    left = gated[:, s * piece:(s + 1) * piece]
                else:
                    gate = times(normed[...], ("gate", e, s))
                    done(("gate", e, s))
                    up = times(normed[...], ("up", e, s))
                    done(("up", e, s))
                    left = activated(gate, up, e)
                if first:
                    part[...] = times(left, ("down", e, s))
                else:
                    part[...] += times(left, ("down", e, s))
                first = False
                done(("down", e, s))
        keep_ref[...] = part[0:rows, :]
        send_ref[...] = part[half_rows:half_rows + rows, :].astype(BF16)


def split_rows_kernel(places, local, held_ref, keep_ref, got_ref, rows_ref, held_out, *outs):
    place, _ = position()
    rows = keep_ref.shape[0]
    total = (keep_ref[...] + got_ref[...].astype(F32)).astype(BF16)
    for k in range(1, places):
        outs[k][...] = jnp.dot(
            picker(place ^ k, rows, local), total, preferred_element_type=F32
        ).astype(BF16)
    pick = picker(place, rows, local)
    outs[0][...] = jnp.dot(pick, total, preferred_element_type=F32) + jnp.dot(
        pick, rows_ref[...], preferred_element_type=F32
    )


def last_kernel(places, *refs):
    own_ref, chunks, before_ref, out_ref = refs[0], refs[1:places], refs[places], refs[places + 1]
    total = own_ref[...]
    for chunk in chunks:
        total = total + chunk[...].astype(F32)
    last = lax.axis_index("section") == lax.axis_size("section") - 1
    result = jnp.where(last, total, before_ref[...].astype(F32)).astype(BF16)
    micro, local_rows, _ = out_ref.shape
    for m in range(micro):
        out_ref[m] = result[m * local_rows:(m + 1) * local_rows, :]


def on_device(inputs, gain, w_gate, w_up, w_down, routes, shares):
    sections = lax.axis_size("section")
    places = lax.axis_size("fsdp") // 2
    micro, local_rows, width = inputs.shape
    _, experts, _, hidden = w_gate.shape
    local = micro * local_rows
    rows = places * local
    half_rows = round_up(rows, 64)
    across = places
    while (width // across) % 128 or width % across:
        across //= 2
    block = (rows // (places // across), width // across)
    resident = min(experts, RESIDENT_BYTES // (4 * width * hidden))
    half = lax.axis_index("fsdp") % 2

    def by_half(array):
        cut = array[0].reshape(micro, places, 2, local_rows, -1)
        return cut.transpose(2, 1, 0, 3, 4).reshape(2, rows, -1)

    chosen = by_half(routes)[..., None] == jnp.arange(experts, dtype=jnp.int32)
    comb = jnp.sum(jnp.where(chosen, by_half(shares)[..., None], 0.0), axis=2)
    comb = jnp.where(half == 0, comb, comb[::-1])
    comb = jnp.pad(comb, ((0, 0), (0, half_rows - rows), (0, 0))).reshape(2 * half_rows, experts)

    def swapped(array):
        return moved(array, sections, places, lambda s, p, c: (s, p, 1 - c))

    def within(array, k):
        return moved(array, sections, places, lambda s, p, c: (s, p ^ k, c))

    def onward(array, tick, k, leg):
        def target(section, place, half):
            if section != ring_of(tick, sections, half)[leg]:
                return None
            return (after(tick, sections, half, section), place ^ k, half)

        return moved(array, sections, places, target)

    def like(shape, dtype=BF16):
        return jax.ShapeDtypeStruct(shape, dtype)

    entry = jnp.pad(inputs.reshape(local, width), ((0, SLOT_ROWS - local), (0, 0)))
    pieces = [entry] + [within(entry, k) for k in range(1, places)]
    held = hold(w_gate, w_up, comb, resident)
    held, mine = chained(
        functools.partial(entry_kernel, places, local), [like((rows, width))], pieces, held
    )
    own = entry
    stream_flops = 6 * 2 * half_rows * width * hidden * experts
    stream_bytes = 2 * 3 * width * hidden * experts - 4 * width * hidden * resident
    for tick in range(sections):
        other = swapped(mine)
        held, keep, send = chained(
            functools.partial(layer_kernel, tick, resident, half_rows),
            [like((rows, width), F32), like((rows, width))],
            [mine, other, gain, comb, w_gate, w_up, w_down],
            held,
            specs=[VMEM, VMEM, VMEM, VMEM, HBM, HBM, HBM],
            scratch=[
                pltpu.VMEM((2 * half_rows, width), BF16),
                pltpu.VMEM((2 * half_rows, width), F32),
                pltpu.VMEM((GATE_SLOTS, width, hidden // 2), BF16),
                pltpu.VMEM((DOWN_SLOTS, hidden // 2, width), BF16),
                pltpu.SemaphoreType.DMA((GATE_SLOTS,)),
                pltpu.SemaphoreType.DMA((DOWN_SLOTS,)),
            ],
            pinned=2,
            flops=stream_flops,
            moved_bytes=stream_bytes,
        )
        got = swapped(send)
        if tick + 1 == sections:
            break
        held, *blocks = chained(
            functools.partial(split_kernel, places, across),
            [like(block)] * places, [keep, got, mine], held,
        )
        blocks = [onward(blocks[places - 1 - k], tick, k, 0) for k in reversed(range(places))]
        held, summed = chained(
            functools.partial(add_kernel, places), [like(block)], blocks, held
        )
        blocks = [onward(summed, tick, k, 1) for k in reversed(range(places))][::-1]
        held, mine, own = chained(
            functools.partial(join_kernel, places, across, local, tick + 1),
            [like((rows, width)), like((SLOT_ROWS, width))], blocks + [own], held,
        )
    before = moved(own, sections, places, lambda s, p, c: ((s - 1) % sections, p, c))
    held, *pieces = chained(
        functools.partial(split_rows_kernel, places, local),
        [like((SLOT_ROWS, width), F32)] + [like((SLOT_ROWS, width))] * (places - 1),
        [keep, got, mine], held,
    )
    pieces = [pieces[0]] + [within(pieces[k], k) for k in range(1, places)]
    result = pl.pallas_call(
        functools.partial(last_kernel, places),
        out_shape=like((micro, local_rows, width)),
        in_specs=[VMEM] * (places + 1),
        out_specs=VMEM,
    )(*[pltpu.with_memory_space_constraint(array, pltpu.VMEM) for array in (*pieces, before)])
    return result[None]


def solution(mesh):
    placed = (
        P(None, "fsdp", None),
        P("section", None),
        P("section", None, None, "fsdp"),
        P("section", None, None, "fsdp"),
        P("section", None, "fsdp", None),
        P("section", None, None, None),
        P("section", None, None, None),
    )
    return jax.shard_map(
        on_device,
        mesh=mesh,
        in_specs=placed,
        out_specs=P("section", None, "fsdp", None),
        check_vma=False,
    )
```

```python
import functools

import jax
import jax.numpy as jnp
from jax import lax
from jax.experimental import pallas as pl
from jax.experimental.pallas import tpu as pltpu
from jax.sharding import PartitionSpec as P

F32 = jnp.float32
BF16 = jnp.bfloat16
MESH_AXES = ("section", "fsdp")
RESIDENT_BYTES = 36 * 2**20
SCOPED_BYTES = 24 * 2**20
DOWN_SLOTS = 4

GATE_SLOTS = 2
VMEM = pl.BlockSpec(memory_space=pltpu.VMEM)
HBM = pl.BlockSpec(memory_space=pl.ANY)


def round_up(value, to):
    return (value + to - 1) // to * to


def moved(array, sections, places, target):
    pairs = []
    for section in range(sections):
        for place in range(places):
            for half in range(2):
                goal = target(section, place, half)
                if goal is None:
                    continue
                to_section, to_place, to_half = goal
                pairs.append(
                    (
                        (section * places + place) * 2 + half,
                        (to_section * places + to_place) * 2 + to_half,
                    )
                )
    return lax.ppermute(array, MESH_AXES, pairs)


def ring_of(tick, sections, half):
    others = [s for s in range(sections) if s not in (tick, tick + 1)]
    helper = others[half % len(others)]
    return [tick, helper, tick + 1] + [s for s in others if s != helper]


def after(tick, sections, half, section):
    ring = ring_of(tick, sections, half)
    return ring[(ring.index(section) + 1) % sections]


def position():
    index = lax.axis_index("fsdp")
    return index // 2, index % 2


def chained(kernel, outs, ins, held, specs=None, scratch=(), pinned=99, flops=0,
            moved_bytes=0):
    specs = [VMEM] * len(ins) if specs is None else specs
    ins = [
        pltpu.with_memory_space_constraint(array, pltpu.VMEM)
        if spec is VMEM and i < pinned
        else array
        for i, (array, spec) in enumerate(zip(ins, specs, strict=True))
    ]
    result = pl.pallas_call(
        kernel,
        out_shape=tuple(
            pltpu.VMEM(out.shape, out.dtype) for out in (held, *outs)
        ),
        in_specs=[VMEM] + list(specs),
        out_specs=(VMEM,) * (len(outs) + 1),
        input_output_aliases={0: 0},
        scratch_shapes=list(scratch),
        compiler_params=pltpu.CompilerParams(vmem_limit_bytes=SCOPED_BYTES),
        cost_estimate=pl.CostEstimate(
            flops=flops, bytes_accessed=moved_bytes, transcendentals=0
        ),
    )(held, *ins)
    return result


def arranged(comb_ref, rows, half_rows, local_rows):
    places = lax.axis_size("fsdp") // 2
    tokens, local = 2 * places * local_rows, rows // places
    _, half = position()
    shape = (2 * half_rows, comb_ref.shape[0])
    row = lax.broadcasted_iota(jnp.int32, shape, 0)
    index = lax.broadcasted_iota(jnp.int32, shape, 1)
    micro, token = lax.div(index, tokens), lax.rem(index, tokens)
    owner, within = lax.div(token, local_rows), lax.rem(token, local_rows)
    place, side = lax.div(owner, 2), lax.rem(owner, 2)
    goal = place * local + micro * local_rows + within
    goal = goal + jnp.where(side == half, 0, half_rows)
    return jnp.dot(
        (row == goal).astype(F32), comb_ref[...], precision=lax.Precision.HIGHEST,
        preferred_element_type=F32,
    )


def hold_kernel(resident, rows, local_rows, gate_ref, up_ref, comb_ref, held_ref, arranged_ref, sems,
                comb, ordered, comb_sems):
    copies = []
    for expert in range(resident):
        for which, ref in ((0, gate_ref), (1, up_ref)):
            slot = which * resident + expert
            copies.append(
                pltpu.make_async_copy(ref.at[0, expert], held_ref.at[slot], sems.at[slot])
            )
    comb_copy = pltpu.make_async_copy(comb_ref, comb, comb_sems.at[0])
    ordered_copy = pltpu.make_async_copy(ordered, arranged_ref, comb_sems.at[1])
    for copy in [comb_copy] + copies:
        copy.start()
    comb_copy.wait()
    ordered[...] = arranged(comb, rows, ordered.shape[0] // 2, local_rows)
    ordered_copy.start()
    for copy in copies + [ordered_copy]:
        copy.wait()


def hold(w_gate, w_up, comb, resident, rows, half_rows, local_rows):
    _, experts, width, hidden = w_gate.shape
    shape = (2 * resident, width, hidden)
    return pl.pallas_call(
        functools.partial(hold_kernel, resident, rows, local_rows),
        out_shape=(
            pltpu.VMEM(shape, BF16),
            jax.ShapeDtypeStruct((2 * half_rows, experts), F32),
        ),
        in_specs=[HBM, HBM, HBM],
        out_specs=(VMEM, HBM),
        scratch_shapes=[
            pltpu.SemaphoreType.DMA((2 * resident,)),
            pltpu.VMEM(comb.shape, F32),
            pltpu.VMEM((2 * half_rows, experts), F32),
            pltpu.SemaphoreType.DMA((2,)),
        ],
        compiler_params=pltpu.CompilerParams(vmem_limit_bytes=SCOPED_BYTES),
        cost_estimate=pl.CostEstimate(
            flops=0, bytes_accessed=2 * 2 * resident * width * hidden, transcendentals=0
        ),
    )(w_gate, w_up, comb)


def packed(place, rows, local, array):
    row = lax.broadcasted_iota(jnp.int32, (2 * local, rows), 0)
    column = lax.broadcasted_iota(jnp.int32, (2 * local, rows), 1)
    left = (column == place * local + row).astype(BF16)
    left = jnp.where(row < local, left, jnp.zeros_like(left))
    right = (column == (place - 1) * local + row).astype(BF16)
    right = jnp.where(row >= local, right, jnp.zeros_like(right))
    middle = array.shape[1] // 2
    return jnp.dot(left, array[:, :middle], preferred_element_type=F32) + jnp.dot(
        right, array[:, middle:], preferred_element_type=F32
    )


def entry_kernel(places, held_ref, *refs):
    chunks, out_ref, own_ref = refs[:places], refs[places + 1], refs[places + 2]
    own_ref[...] = jnp.zeros_like(own_ref)
    place, _ = position()
    micro, local_rows, _ = chunks[0].shape
    rows, local = out_ref.shape[0], micro * local_rows
    column = lax.broadcasted_iota(jnp.int32, (local, rows), 1)
    row = lax.broadcasted_iota(jnp.int32, (local, rows), 0)
    picks = [(column == (place ^ k) * local + row).astype(F32) for k in range(places)]
    pieces = [chunk[m].astype(F32) for chunk in chunks for m in range(micro)]
    out_ref[...] = lax.dot_general(
        jnp.concatenate(picks, axis=0).astype(BF16),
        jnp.concatenate(pieces, axis=0).astype(BF16),
        (((0,), (0,)), ((), ())),
        preferred_element_type=F32,
    ).astype(BF16)


def block_at(ref, place, rows, columns, across):
    if across * columns == ref.shape[1] and rows == ref.shape[0]:
        row_start = 0
    else:
        row_start = pl.multiple_of(place // across * rows, 16)
    column_start = pl.multiple_of(place % across * columns, 128)
    return (pl.ds(row_start, rows), pl.ds(column_start, columns))


def split_kernel(places, across, held_ref, keep_ref, got_ref, rows_ref, held_out, *outs):
    place, _ = position()
    for k in range(places):
        out = outs[places - 1 - k]
        at = block_at(keep_ref, place ^ k, out.shape[0], out.shape[1], across)
        total = keep_ref[at] + got_ref[at].astype(F32)
        if k == 0:
            total = total + rows_ref[at].astype(F32)
        out[...] = total.astype(BF16)


def add_kernel(places, held_ref, *refs):
    total = refs[0][...].astype(F32)
    for k in range(1, places):
        total = total + refs[k][...].astype(F32)
    refs[places + 1][...] = total.astype(BF16)


def join_kernel(places, across, local, tick, held_ref, *refs):
    chunks, own_ref, out_ref, new_own_ref = (
        refs[:places], refs[places], refs[places + 2], refs[places + 3],
    )
    place, _ = position()
    for k in range(places):
        chunk = chunks[k]
        at = block_at(out_ref, place ^ k, chunk.shape[0], chunk.shape[1], across)
        out_ref[at] = chunk[...]

    active = lax.axis_index("section") == tick

    @pl.when(active)
    def _():
        new_own_ref[...] = packed(place, out_ref.shape[0], local, out_ref[...]).astype(BF16)

    @pl.when(jnp.logical_not(active))
    def _():
        new_own_ref[...] = own_ref[...]


def layer_kernel(tick, resident, half_rows, held_ref, mine_ref, other_ref, gain_ref, comb_ref, gate_ref,
                 up_ref, down_ref, held_out, keep_ref, send_ref, normed, part, gate_slots, down_slots,
                 gate_sems, down_sems):
    experts = gate_ref.shape[1]
    hidden = gate_ref.shape[3]
    piece = hidden // 2
    rows = mine_ref.shape[0]

    @pl.when(lax.axis_index("section") == tick)
    def _():
        queue = []
        for e in range(resident):
            queue += [("down", e, 0), ("down", e, 1)]
        for e in range(resident, experts):
            queue += [("gate", e, 0), ("up", e, 0), ("down", e, 0), ("down", e, 1),
                      ("gate", e, 1), ("up", e, 1)]
        numbers, counts = {}, {"down": 0, "gate": 0}
        for kind, e, s in queue:
            pool = "down" if kind == "down" else "gate"
            numbers[kind, e, s] = (pool, counts[pool])
            counts[pool] += 1
        slots = {"down": DOWN_SLOTS, "gate": GATE_SLOTS}
        freed = {"down": 0, "gate": 0}
        pending = list(queue)

        def copy_of(item):
            kind, e, s = item
            pool, number = numbers[item]
            slot = number % slots[pool]
            cut = pl.ds(s * piece, piece)
            if kind == "down":
                return pltpu.make_async_copy(
                    down_ref.at[0, e, cut, :], down_slots.at[slot], down_sems.at[slot]
                ), down_slots.at[slot]
            source = gate_ref if kind == "gate" else up_ref
            return pltpu.make_async_copy(
                source.at[0, e, :, cut], gate_slots.at[slot], gate_sems.at[slot]
            ), gate_slots.at[slot]

        def issue():
            while pending:
                pool, number = numbers[pending[0]]
                if number >= freed[pool] + slots[pool]:
                    return
                copy_of(pending.pop(0))[0].start()

        def times(left, item):
            copy, ref = copy_of(item)
            copy.wait()
            result = jnp.dot(left, ref[...], preferred_element_type=F32)
            return result

        def done(item):
            freed[numbers[item][0]] += 1
            issue()

        issue()
        for ref, start in ((mine_ref, 0), (other_ref, half_rows)):
            values = ref[...].astype(F32)
            scale = lax.rsqrt(jnp.mean(values * values, axis=-1, keepdims=True) + 1e-05)
            normed[start:start + rows, :] = (values * scale * gain_ref[...]).astype(BF16)
            if half_rows > rows:
                normed[start + rows:start + half_rows, :] = jnp.zeros(
                    (half_rows - rows, values.shape[1]), BF16
                )

        def activated(gate, up, e):
            return (gate / (1.0 + jnp.exp(-gate)) * up * comb_ref[:, e:e + 1]).astype(BF16)

        first = True
        for e in range(experts):
            if e < resident:
                gate = jnp.dot(normed[...], held_ref[e], preferred_element_type=F32)
                up = jnp.dot(normed[...], held_ref[resident + e], preferred_element_type=F32)
                gated = activated(gate, up, e)
            for s in range(2):
                if e < resident:
                    left = gated[:, s * piece:(s + 1) * piece]
                else:
                    gate = times(normed[...], ("gate", e, s))
                    done(("gate", e, s))
                    up = times(normed[...], ("up", e, s))
                    done(("up", e, s))
                    left = activated(gate, up, e)
                if first:
                    part[...] = times(left, ("down", e, s))
                else:
                    part[...] += times(left, ("down", e, s))
                first = False
                done(("down", e, s))
        keep_ref[...] = part[0:rows, :]
        send_ref[...] = part[half_rows:half_rows + rows, :].astype(BF16)


def split_rows_kernel(places, local, held_ref, keep_ref, got_ref, rows_ref, held_out, *outs):
    place, _ = position()
    rows = keep_ref.shape[0]
    total = (keep_ref[...] + got_ref[...].astype(F32)).astype(BF16)
    for k in range(1, places):
        outs[places - k][...] = packed(place ^ k, rows, local, total).astype(BF16)
    outs[0][...] = packed(place, rows, local, total) + packed(place, rows, local, rows_ref[...])


def last_kernel(places, *refs):
    own_ref, chunks, before_ref, out_ref = refs[0], refs[1:places], refs[places], refs[places + 1]
    total = own_ref[...]
    for chunk in chunks:
        total = total + chunk[...].astype(F32)
    last = lax.axis_index("section") == lax.axis_size("section") - 1
    result = jnp.where(last, total, before_ref[...].astype(F32))
    micro, local_rows, width = out_ref.shape
    for m in range(micro):
        for side in range(2):
            start = (side * micro + m) * local_rows
            columns = slice(side * width // 2, (side + 1) * width // 2)
            out_ref[m, :, columns] = result[start:start + local_rows, :].astype(BF16)


def on_device(inputs, gain, w_gate, w_up, w_down, routes, shares):
    sections = lax.axis_size("section")
    places = lax.axis_size("fsdp") // 2
    micro, local_rows, width = inputs.shape
    _, experts, _, hidden = w_gate.shape
    local = micro * local_rows
    rows = places * local
    half_rows = round_up(rows, 64)
    across = places
    while (width // across) % 128 or width % across:
        across //= 2
    block = (rows // (places // across), width // across)
    resident = min(experts, RESIDENT_BYTES // (4 * width * hidden))

    chosen = routes[0][..., None] == jnp.arange(experts, dtype=jnp.int32)
    comb = jnp.sum(jnp.where(chosen, shares[0][..., None], 0.0), axis=2).reshape(-1, experts)

    def swapped(array):
        return moved(array, sections, places, lambda s, p, c: (s, p, 1 - c))

    def within(array, k):
        return moved(array, sections, places, lambda s, p, c: (s, p ^ k, c))

    def full(leg, k):
        return k == places - 2 if leg == 0 else k < 3 and k < places - 1

    def onward(array, tick, k, leg):
        def target(section, place, half):
            if not full(leg, k) and section != ring_of(tick, sections, half)[leg]:
                return None
            return (after(tick, sections, half, section), place ^ k, half)

        return moved(array, sections, places, target)

    def like(shape, dtype=BF16):
        return jax.ShapeDtypeStruct(shape, dtype)

    pieces = [inputs] + [within(inputs, k) for k in range(1, places)]
    held, comb = hold(w_gate, w_up, comb, resident, rows, half_rows, local_rows)
    slot = (2 * local, width // 2)
    held, mine, own = chained(
        functools.partial(entry_kernel, places),
        [like((rows, width)), like(slot)], pieces, held,
    )
    stream_flops = 6 * 2 * half_rows * width * hidden * experts
    stream_bytes = 2 * 3 * width * hidden * experts - 4 * width * hidden * resident
    for tick in range(sections):
        other = swapped(mine)
        held, keep, send = chained(
            functools.partial(layer_kernel, tick, resident, half_rows),
            [like((rows, width), F32), like((rows, width))],
            [mine, other, gain, comb, w_gate, w_up, w_down],
            held,
            specs=[VMEM, VMEM, VMEM, VMEM, HBM, HBM, HBM],
            scratch=[
                pltpu.VMEM((2 * half_rows, width), BF16),
                pltpu.VMEM((2 * half_rows, width), F32),
                pltpu.VMEM((GATE_SLOTS, width, hidden // 2), BF16),
                pltpu.VMEM((DOWN_SLOTS, hidden // 2, width), BF16),
                pltpu.SemaphoreType.DMA((GATE_SLOTS,)),
                pltpu.SemaphoreType.DMA((DOWN_SLOTS,)),
            ],
            pinned=2,
            flops=stream_flops,
            moved_bytes=stream_bytes,
        )
        got = swapped(send)
        if tick + 1 == sections:
            break
        held, *blocks = chained(
            functools.partial(split_kernel, places, across),
            [like(block)] * places, [keep, got, mine], held,
        )
        blocks = [onward(blocks[places - 1 - k], tick, k, 0) for k in reversed(range(places))]
        held, summed = chained(
            functools.partial(add_kernel, places), [like(block)], blocks, held
        )
        blocks = [onward(summed, tick, k, 1) for k in reversed(range(places))][::-1]
        held, mine, own = chained(
            functools.partial(join_kernel, places, across, local, tick + 1),
            [like((rows, width)), like(slot)], blocks + [own], held,
        )
    before = moved(own, sections, places, lambda s, p, c: ((s - 1) % sections, p, c))
    held, *pieces = chained(
        functools.partial(split_rows_kernel, places, local),
        [like(slot, F32)] + [like(slot)] * (places - 1),
        [keep, got, mine], held,
    )
    pieces = [pieces[0]] + [within(pieces[places - k], k) for k in reversed(range(1, places))]
    result = pl.pallas_call(
        functools.partial(last_kernel, places),
        out_shape=like((micro, local_rows, width)),
        in_specs=[VMEM] * (places + 1),
        out_specs=VMEM,
    )(*[pltpu.with_memory_space_constraint(array, pltpu.VMEM) for array in (*pieces, before)])
    return result[None]


def solution(mesh):
    placed = (
        P(None, "fsdp", None),
        P("section", None),
        P("section", None, None, "fsdp"),
        P("section", None, None, "fsdp"),
        P("section", None, "fsdp", None),
        P("section", None, None, None),
        P("section", None, None, None),
    )
    return jax.shard_map(
        on_device,
        mesh=mesh,
        in_specs=placed,
        out_specs=P("section", None, "fsdp", None),
        check_vma=False,
    )
```

```python
import functools

import jax
import jax.numpy as jnp
from jax import lax
from jax.experimental import pallas as pl
from jax.experimental.pallas import tpu as pltpu
from jax.sharding import PartitionSpec as P

F32 = jnp.float32
BF16 = jnp.bfloat16
MESH_AXES = ("section", "fsdp")
RESIDENT_BYTES = 36 * 2**20
SCOPED_BYTES = 24 * 2**20
DOWN_SLOTS = 4

GATE_SLOTS = 2
VMEM = pl.BlockSpec(memory_space=pltpu.VMEM)
HBM = pl.BlockSpec(memory_space=pl.ANY)


def round_up(value, to):
    return (value + to - 1) // to * to


def moved(array, sections, places, target):
    pairs = []
    for section in range(sections):
        for place in range(places):
            for half in range(2):
                goal = target(section, place, half)
                if goal is None:
                    continue
                to_section, to_place, to_half = goal
                pairs.append(
                    (
                        (section * places + place) * 2 + half,
                        (to_section * places + to_place) * 2 + to_half,
                    )
                )
    return lax.ppermute(array, MESH_AXES, pairs)


def ring_of(tick, sections, half):
    others = [s for s in range(sections) if s not in (tick, tick + 1)]
    helper = others[half % len(others)]
    return [tick, helper, tick + 1] + [s for s in others if s != helper]


def after(tick, sections, half, section):
    ring = ring_of(tick, sections, half)
    return ring[(ring.index(section) + 1) % sections]


def position():
    index = lax.axis_index("fsdp")
    return index // 2, index % 2


def chained(kernel, outs, ins, held, specs=None, scratch=(), pinned=99, flops=0,
            moved_bytes=0):
    specs = [VMEM] * len(ins) if specs is None else specs
    ins = [
        pltpu.with_memory_space_constraint(array, pltpu.VMEM)
        if spec is VMEM and i < pinned
        else array
        for i, (array, spec) in enumerate(zip(ins, specs, strict=True))
    ]
    result = pl.pallas_call(
        kernel,
        out_shape=tuple(
            pltpu.VMEM(out.shape, out.dtype) for out in (held, *outs)
        ),
        in_specs=[VMEM] + list(specs),
        out_specs=(VMEM,) * (len(outs) + 1),
        input_output_aliases={0: 0},
        scratch_shapes=list(scratch),
        compiler_params=pltpu.CompilerParams(vmem_limit_bytes=SCOPED_BYTES),
        cost_estimate=pl.CostEstimate(
            flops=flops, bytes_accessed=moved_bytes, transcendentals=0
        ),
    )(held, *ins)
    return result


def arranged(comb_ref, rows, half_rows, local_rows):
    places = lax.axis_size("fsdp") // 2
    micro_count, _, tokens = comb_ref.shape
    local = rows // places
    _, half = position()
    shape = (2 * half_rows, tokens)
    row = lax.broadcasted_iota(jnp.int32, shape, 0)
    token = lax.broadcasted_iota(jnp.int32, shape, 1)
    owner, within = lax.div(token, local_rows), lax.rem(token, local_rows)
    place, side = lax.div(owner, 2), lax.rem(owner, 2)
    goal = place * local + within + jnp.where(side == half, 0, half_rows)
    total = None
    for micro in range(micro_count):
        part = lax.dot_general(
            (row == goal + micro * local_rows).astype(F32), comb_ref[micro],
            (((1,), (1,)), ((), ())), precision=lax.Precision.HIGHEST, preferred_element_type=F32,
        )
        total = part if total is None else total + part
    return total


def hold_kernel(resident, rows, local_rows, gate_ref, up_ref, comb_ref, held_ref, arranged_ref, sems,
                comb, ordered, comb_sems):
    copies = []
    for expert in range(resident):
        for which, ref in ((0, gate_ref), (1, up_ref)):
            slot = which * resident + expert
            if slot < 2 * resident - 1:
                copies.append(
                    pltpu.make_async_copy(ref.at[0, expert], held_ref.at[slot], sems.at[slot])
                )
    comb_copy = pltpu.make_async_copy(comb_ref, comb, comb_sems.at[0])
    ordered_copy = pltpu.make_async_copy(ordered, arranged_ref, comb_sems.at[1])
    for copy in [comb_copy] + copies:
        copy.start()
    comb_copy.wait()
    ordered[...] = arranged(comb, rows, ordered.shape[0] // 2, local_rows)
    ordered_copy.start()
    for copy in copies + [ordered_copy]:
        copy.wait()


def hold(w_gate, w_up, comb, resident, rows, half_rows, local_rows):
    _, experts, width, hidden = w_gate.shape
    shape = (2 * resident, width, hidden)
    return pl.pallas_call(
        functools.partial(hold_kernel, resident, rows, local_rows),
        out_shape=(
            pltpu.VMEM(shape, BF16),
            jax.ShapeDtypeStruct((2 * half_rows, experts), F32),
        ),
        in_specs=[HBM, HBM, HBM],
        out_specs=(VMEM, HBM),
        scratch_shapes=[
            pltpu.SemaphoreType.DMA((2 * resident,)),
            pltpu.VMEM(comb.shape, F32),
            pltpu.VMEM((2 * half_rows, experts), F32),
            pltpu.SemaphoreType.DMA((2,)),
        ],
        compiler_params=pltpu.CompilerParams(vmem_limit_bytes=SCOPED_BYTES),
        cost_estimate=pl.CostEstimate(
            flops=0, bytes_accessed=2 * 2 * resident * width * hidden, transcendentals=0
        ),
    )(w_gate, w_up, comb)


def packed(place, rows, local, array):
    row = lax.broadcasted_iota(jnp.int32, (2 * local, rows), 0)
    column = lax.broadcasted_iota(jnp.int32, (2 * local, rows), 1)
    left = (column == place * local + row).astype(BF16)
    left = jnp.where(row < local, left, jnp.zeros_like(left))
    right = (column == (place - 1) * local + row).astype(BF16)
    right = jnp.where(row >= local, right, jnp.zeros_like(right))
    middle = array.shape[1] // 2
    return jnp.dot(left, array[:, :middle], preferred_element_type=F32) + jnp.dot(
        right, array[:, middle:], preferred_element_type=F32
    )


def entry_kernel(places, held_ref, *refs):
    chunks, out_ref, own_ref = refs[:places], refs[places + 1], refs[places + 2]
    own_ref[...] = jnp.zeros_like(own_ref)
    place, _ = position()
    micro, local_rows, _ = chunks[0].shape
    rows, local = out_ref.shape[0], micro * local_rows
    column = lax.broadcasted_iota(jnp.int32, (local, rows), 1)
    row = lax.broadcasted_iota(jnp.int32, (local, rows), 0)
    picks = [(column == (place ^ k) * local + row).astype(F32) for k in range(places)]
    pieces = [chunk[m].astype(F32) for chunk in chunks for m in range(micro)]
    out_ref[...] = lax.dot_general(
        jnp.concatenate(picks, axis=0).astype(BF16),
        jnp.concatenate(pieces, axis=0).astype(BF16),
        (((0,), (0,)), ((), ())),
        preferred_element_type=F32,
    ).astype(BF16)


def block_at(ref, place, rows, columns, across):
    if across * columns == ref.shape[1] and rows == ref.shape[0]:
        row_start = 0
    else:
        row_start = pl.multiple_of(place // across * rows, 16)
    column_start = pl.multiple_of(place % across * columns, 128)
    return (pl.ds(row_start, rows), pl.ds(column_start, columns))


def split_kernel(places, across, held_ref, keep_ref, got_ref, rows_ref, held_out, *outs):
    place, _ = position()
    for k in range(places):
        out = outs[places - 1 - k]
        at = block_at(keep_ref, place ^ k, out.shape[0], out.shape[1], across)
        total = keep_ref[at] + got_ref[at].astype(F32)
        if k == 0:
            total = total + rows_ref[at].astype(F32)
        out[...] = total.astype(BF16)


def add_kernel(places, held_ref, *refs):
    total = refs[0][...].astype(F32)
    for k in range(1, places):
        total = total + refs[k][...].astype(F32)
    refs[places + 1][...] = total.astype(BF16)


def join_kernel(places, across, local, tick, held_ref, *refs):
    chunks, own_ref, out_ref, new_own_ref = (
        refs[:places], refs[places], refs[places + 2], refs[places + 3],
    )
    place, _ = position()
    for k in range(places):
        chunk = chunks[k]
        at = block_at(out_ref, place ^ k, chunk.shape[0], chunk.shape[1], across)
        out_ref[at] = chunk[...]

    active = lax.axis_index("section") == tick

    @pl.when(active)
    def _():
        new_own_ref[...] = packed(place, out_ref.shape[0], local, out_ref[...]).astype(BF16)

    @pl.when(jnp.logical_not(active))
    def _():
        new_own_ref[...] = own_ref[...]


def layer_kernel(tick, resident, half_rows, held_ref, mine_ref, other_ref, gain_ref, comb_ref, gate_ref,
                 up_ref, down_ref, held_out, keep_ref, send_ref, normed, part, gate_slots, down_slots,
                 gate_sems, down_sems, held_sem):
    experts = gate_ref.shape[1]
    hidden = gate_ref.shape[3]
    piece = hidden // 2
    rows = mine_ref.shape[0]

    active = lax.axis_index("section") == tick
    last_held = pltpu.make_async_copy(
        up_ref.at[0, resident - 1], held_out.at[2 * resident - 1], held_sem
    )
    if tick == 0:
        @pl.when(jnp.logical_not(active))
        def _():
            last_held.start()
            last_held.wait()

    @pl.when(active)
    def _():
        work = [(e, (0, 1)) for e in range(resident)]
        streamed = [(e, (s,)) for e in range(resident, experts) for s in range(2)]
        work = work[:-1] + streamed[:-1] + work[-1:] + streamed[-1:]
        queue = []
        for e, halves in work:
            for s in halves:
                if e >= resident:
                    queue += [("gate", e, s), ("up", e, s)]
                queue += [("down", e, s)]
        numbers, counts = {}, {"down": 0, "gate": 0}
        for kind, e, s in queue:
            pool = "down" if kind == "down" else "gate"
            numbers[kind, e, s] = (pool, counts[pool])
            counts[pool] += 1
        slots = {"down": DOWN_SLOTS, "gate": GATE_SLOTS}
        freed = {"down": 0, "gate": 0}
        pending = list(queue)

        def copy_of(item):
            kind, e, s = item
            pool, number = numbers[item]
            slot = number % slots[pool]
            cut = pl.ds(s * piece, piece)
            if kind == "down":
                return pltpu.make_async_copy(
                    down_ref.at[0, e, cut, :], down_slots.at[slot], down_sems.at[slot]
                ), down_slots.at[slot]
            source = gate_ref if kind == "gate" else up_ref
            return pltpu.make_async_copy(
                source.at[0, e, :, cut], gate_slots.at[slot], gate_sems.at[slot]
            ), gate_slots.at[slot]

        def issue():
            while pending:
                pool, number = numbers[pending[0]]
                if number >= freed[pool] + slots[pool]:
                    return
                copy_of(pending.pop(0))[0].start()

        def times(left, item):
            copy, ref = copy_of(item)
            copy.wait()
            result = jnp.dot(left, ref[...], preferred_element_type=F32)
            return result

        def done(item):
            freed[numbers[item][0]] += 1
            issue()

        issue()
        for ref, start in ((mine_ref, 0), (other_ref, half_rows)):
            values = ref[...].astype(F32)
            scale = lax.rsqrt(jnp.mean(values * values, axis=-1, keepdims=True) + 1e-05)
            normed[start:start + rows, :] = (values * scale * gain_ref[...]).astype(BF16)
            if half_rows > rows:
                normed[start + rows:start + half_rows, :] = jnp.zeros(
                    (half_rows - rows, values.shape[1]), BF16
                )

        def activated(gate, up, e):
            return (gate / (1.0 + jnp.exp(-gate)) * up * comb_ref[:, e:e + 1]).astype(BF16)

        first = True
        for e, halves in work:
            if e < resident:
                gate = jnp.dot(normed[...], held_ref[e], preferred_element_type=F32)
                if tick == 0 and e == resident - 1:
                    last_held.wait()
                up = jnp.dot(normed[...], held_out[resident + e], preferred_element_type=F32)
                gated = activated(gate, up, e)
            for s in halves:
                if e < resident:
                    left = gated[:, s * piece:(s + 1) * piece]
                else:
                    gate = times(normed[...], ("gate", e, s))
                    done(("gate", e, s))
                    up = times(normed[...], ("up", e, s))
                    done(("up", e, s))
                    left = activated(gate, up, e)
                if first:
                    part[...] = times(left, ("down", e, s))
                else:
                    part[...] += times(left, ("down", e, s))
                if first and tick == 0:
                    last_held.start()
                first = False
                done(("down", e, s))
        keep_ref[...] = part[0:rows, :]
        send_ref[...] = part[half_rows:half_rows + rows, :].astype(BF16)


def split_rows_kernel(places, local, held_ref, keep_ref, got_ref, rows_ref, held_out, *outs):
    place, _ = position()
    rows = keep_ref.shape[0]
    total = (keep_ref[...] + got_ref[...].astype(F32)).astype(BF16)
    for k in range(1, places):
        outs[places - k][...] = packed(place ^ k, rows, local, total).astype(BF16)
    outs[0][...] = packed(place, rows, local, total) + packed(place, rows, local, rows_ref[...])


def last_kernel(places, *refs):
    own_ref, chunks, before_ref, out_ref = refs[0], refs[1:places], refs[places], refs[places + 1]
    total = own_ref[...]
    for chunk in chunks:
        total = total + chunk[...].astype(F32)
    last = lax.axis_index("section") == lax.axis_size("section") - 1
    result = jnp.where(last, total, before_ref[...].astype(F32))
    micro, local_rows, width = out_ref.shape
    for m in range(micro):
        for side in range(2):
            start = (side * micro + m) * local_rows
            columns = slice(side * width // 2, (side + 1) * width // 2)
            out_ref[m, :, columns] = result[start:start + local_rows, :].astype(BF16)


def on_device(inputs, gain, w_gate, w_up, w_down, routes, shares):
    sections = lax.axis_size("section")
    places = lax.axis_size("fsdp") // 2
    micro, local_rows, width = inputs.shape
    _, experts, _, hidden = w_gate.shape
    local = micro * local_rows
    rows = places * local
    half_rows = round_up(rows, 64)
    across = places
    while (width // across) % 128 or width % across:
        across //= 2
    block = (rows // (places // across), width // across)
    resident = min(experts, RESIDENT_BYTES // (4 * width * hidden))

    chosen = routes[0][:, None] == jnp.arange(experts, dtype=jnp.int32)[None, :, None, None]
    comb = jnp.sum(jnp.where(chosen, shares[0][:, None], 0.0), axis=3)

    def swapped(array):
        return moved(array, sections, places, lambda s, p, c: (s, p, 1 - c))

    def within(array, k):
        return moved(array, sections, places, lambda s, p, c: (s, p ^ k, c))

    def full(leg, k):
        return k == places - 1 if leg == 0 else k < 2

    def onward(array, tick, k, leg):
        def target(section, place, half):
            if not full(leg, k) and section != ring_of(tick, sections, half)[leg]:
                return None
            return (after(tick, sections, half, section), place ^ k, half)

        return moved(array, sections, places, target)

    def like(shape, dtype=BF16):
        return jax.ShapeDtypeStruct(shape, dtype)

    pieces = [inputs] + [within(inputs, k) for k in range(1, places)]
    held, comb = hold(w_gate, w_up, comb, resident, rows, half_rows, local_rows)
    slot = (2 * local, width // 2)
    held, mine, own = chained(
        functools.partial(entry_kernel, places),
        [like((rows, width)), like(slot)], pieces, held,
    )
    stream_flops = 6 * 2 * half_rows * width * hidden * experts
    stream_bytes = 2 * 3 * width * hidden * experts - 4 * width * hidden * resident
    for tick in range(sections):
        other = swapped(mine)
        held, keep, send = chained(
            functools.partial(layer_kernel, tick, resident, half_rows),
            [like((rows, width), F32), like((rows, width))],
            [mine, other, gain, comb, w_gate, w_up, w_down],
            held,
            specs=[VMEM, VMEM, VMEM, VMEM, HBM, HBM, HBM],
            scratch=[
                pltpu.VMEM((2 * half_rows, width), BF16),
                pltpu.VMEM((2 * half_rows, width), F32),
                pltpu.VMEM((GATE_SLOTS, width, hidden // 2), BF16),
                pltpu.VMEM((DOWN_SLOTS, hidden // 2, width), BF16),
                pltpu.SemaphoreType.DMA((GATE_SLOTS,)),
                pltpu.SemaphoreType.DMA((DOWN_SLOTS,)),
                pltpu.SemaphoreType.DMA,
            ],
            pinned=2,
            flops=stream_flops,
            moved_bytes=stream_bytes,
        )
        got = swapped(send)
        if tick + 1 == sections:
            break
        held, *blocks = chained(
            functools.partial(split_kernel, places, across),
            [like(block)] * places, [keep, got, mine], held,
        )
        blocks = [onward(blocks[places - 1 - k], tick, k, 0) for k in reversed(range(places))]
        held, summed = chained(
            functools.partial(add_kernel, places), [like(block)], blocks, held
        )
        blocks = [onward(summed, tick, k, 1) for k in reversed(range(places))][::-1]
        held, mine, own = chained(
            functools.partial(join_kernel, places, across, local, tick + 1),
            [like((rows, width)), like(slot)], blocks + [own], held,
        )
    before = moved(own, sections, places, lambda s, p, c: ((s - 1) % sections, p, c))
    held, *pieces = chained(
        functools.partial(split_rows_kernel, places, local),
        [like(slot, F32)] + [like(slot)] * (places - 1),
        [keep, got, mine], held,
    )
    pieces = [pieces[0]] + [within(pieces[places - k], k) for k in reversed(range(1, places))]
    result = pl.pallas_call(
        functools.partial(last_kernel, places),
        out_shape=like((micro, local_rows, width)),
        in_specs=[VMEM] * (places + 1),
        out_specs=VMEM,
    )(*[pltpu.with_memory_space_constraint(array, pltpu.VMEM) for array in (*pieces, before)])
    return result[None]


def solution(mesh):
    placed = (
        P(None, "fsdp", None),
        P("section", None),
        P("section", None, None, "fsdp"),
        P("section", None, None, "fsdp"),
        P("section", None, "fsdp", None),
        P("section", None, None, None),
        P("section", None, None, None),
    )
    return jax.shard_map(
        on_device,
        mesh=mesh,
        in_specs=placed,
        out_specs=P("section", None, "fsdp", None),
        check_vma=False,
    )
```

```python
import functools

import jax
import jax.numpy as jnp
from jax import lax
from jax.experimental import pallas as pl
from jax.experimental.pallas import tpu as pltpu
from jax.sharding import PartitionSpec as P

F32 = jnp.float32
BF16 = jnp.bfloat16
MESH_AXES = ("section", "fsdp")
RESIDENT_BYTES = 36 * 2**20
SCOPED_BYTES = 24 * 2**20
DOWN_SLOTS = 4

GATE_SLOTS = 2
VMEM = pl.BlockSpec(memory_space=pltpu.VMEM)
HBM = pl.BlockSpec(memory_space=pl.ANY)


def round_up(value, to):
    return (value + to - 1) // to * to


def moved(array, sections, places, target):
    pairs = []
    for section in range(sections):
        for place in range(places):
            for half in range(2):
                goal = target(section, place, half)
                if goal is None:
                    continue
                to_section, to_place, to_half = goal
                pairs.append(
                    (
                        (section * places + place) * 2 + half,
                        (to_section * places + to_place) * 2 + to_half,
                    )
                )
    return lax.ppermute(array, MESH_AXES, pairs)


def ring_of(tick, sections, half):
    others = [s for s in range(sections) if s not in (tick, tick + 1)]
    helper = others[half % len(others)]
    return [tick, helper, tick + 1] + [s for s in others if s != helper]


def after(tick, sections, half, section):
    ring = ring_of(tick, sections, half)
    return ring[(ring.index(section) + 1) % sections]


def position():
    index = lax.axis_index("fsdp")
    return index // 2, index % 2


def chained(kernel, outs, ins, held, specs=None, scratch=(), pinned=99, flops=0,
            moved_bytes=0):
    specs = [VMEM] * len(ins) if specs is None else specs
    ins = [
        pltpu.with_memory_space_constraint(array, pltpu.VMEM)
        if spec is VMEM and i < pinned
        else array
        for i, (array, spec) in enumerate(zip(ins, specs, strict=True))
    ]
    result = pl.pallas_call(
        kernel,
        out_shape=tuple(
            pltpu.VMEM(out.shape, out.dtype) for out in (held, *outs)
        ),
        in_specs=[VMEM] + list(specs),
        out_specs=(VMEM,) * (len(outs) + 1),
        input_output_aliases={0: 0},
        scratch_shapes=list(scratch),
        compiler_params=pltpu.CompilerParams(vmem_limit_bytes=SCOPED_BYTES),
        cost_estimate=pl.CostEstimate(
            flops=flops, bytes_accessed=moved_bytes, transcendentals=0
        ),
    )(held, *ins)
    return result


def arranged(comb_ref, rows, half_rows, local_rows):
    places = lax.axis_size("fsdp") // 2
    micro_count, _, tokens = comb_ref.shape
    local = rows // places
    _, half = position()
    shape = (2 * half_rows, tokens)
    row = lax.broadcasted_iota(jnp.int32, shape, 0)
    token = lax.broadcasted_iota(jnp.int32, shape, 1)
    owner, within = lax.div(token, local_rows), lax.rem(token, local_rows)
    place, side = lax.div(owner, 2), lax.rem(owner, 2)
    goal = place * local + within + jnp.where(side == half, 0, half_rows)
    total = None
    for micro in range(micro_count):
        part = lax.dot_general(
            (row == goal + micro * local_rows).astype(F32), comb_ref[micro],
            (((1,), (1,)), ((), ())), precision=lax.Precision.HIGHEST, preferred_element_type=F32,
        )
        total = part if total is None else total + part
    return total


def hold_kernel(resident, rows, local_rows, gate_ref, up_ref, comb_ref, held_ref, arranged_ref, sems,
                comb, ordered, comb_sems):
    copies = []
    for expert in range(resident):
        for which, ref in ((0, gate_ref), (1, up_ref)):
            slot = which * resident + expert
            if slot < 2 * resident - 1:
                copies.append(
                    pltpu.make_async_copy(ref.at[0, expert], held_ref.at[slot], sems.at[slot])
                )
    comb_copy = pltpu.make_async_copy(comb_ref, comb, comb_sems.at[0])
    ordered_copy = pltpu.make_async_copy(ordered, arranged_ref, comb_sems.at[1])
    for copy in [comb_copy] + copies:
        copy.start()
    comb_copy.wait()
    ordered[...] = arranged(comb, rows, ordered.shape[0] // 2, local_rows)
    ordered_copy.start()
    for copy in copies + [ordered_copy]:
        copy.wait()


def hold(w_gate, w_up, comb, resident, rows, half_rows, local_rows):
    _, experts, width, hidden = w_gate.shape
    shape = (2 * resident, width, hidden)
    return pl.pallas_call(
        functools.partial(hold_kernel, resident, rows, local_rows),
        out_shape=(
            pltpu.VMEM(shape, BF16),
            jax.ShapeDtypeStruct((2 * half_rows, experts), F32),
        ),
        in_specs=[HBM, HBM, HBM],
        out_specs=(VMEM, HBM),
        scratch_shapes=[
            pltpu.SemaphoreType.DMA((2 * resident,)),
            pltpu.VMEM(comb.shape, F32),
            pltpu.VMEM((2 * half_rows, experts), F32),
            pltpu.SemaphoreType.DMA((2,)),
        ],
        compiler_params=pltpu.CompilerParams(vmem_limit_bytes=SCOPED_BYTES),
        cost_estimate=pl.CostEstimate(
            flops=0, bytes_accessed=2 * 2 * resident * width * hidden, transcendentals=0
        ),
    )(w_gate, w_up, comb)


def packed(place, rows, local, array):
    row = lax.broadcasted_iota(jnp.int32, (2 * local, rows), 0)
    column = lax.broadcasted_iota(jnp.int32, (2 * local, rows), 1)
    left = (column == place * local + row).astype(BF16)
    left = jnp.where(row < local, left, jnp.zeros_like(left))
    right = (column == (place - 1) * local + row).astype(BF16)
    right = jnp.where(row >= local, right, jnp.zeros_like(right))
    middle = array.shape[1] // 2
    return jnp.dot(left, array[:, :middle], preferred_element_type=F32) + jnp.dot(
        right, array[:, middle:], preferred_element_type=F32
    )


def entry_kernel(places, held_ref, *refs):
    chunks, out_ref, own_ref = refs[:places], refs[places + 1], refs[places + 2]
    own_ref[...] = jnp.zeros_like(own_ref)
    place, _ = position()
    micro, local_rows, _ = chunks[0].shape
    rows, local = out_ref.shape[0], micro * local_rows
    column = lax.broadcasted_iota(jnp.int32, (local, rows), 1)
    row = lax.broadcasted_iota(jnp.int32, (local, rows), 0)
    picks = [(column == (place ^ k) * local + row).astype(F32) for k in range(places)]
    pieces = [chunk[m].astype(F32) for chunk in chunks for m in range(micro)]
    out_ref[...] = lax.dot_general(
        jnp.concatenate(picks, axis=0).astype(BF16),
        jnp.concatenate(pieces, axis=0).astype(BF16),
        (((0,), (0,)), ((), ())),
        preferred_element_type=F32,
    ).astype(BF16)


def block_at(ref, place, rows, columns, across):
    if across * columns == ref.shape[1] and rows == ref.shape[0]:
        row_start = 0
    else:
        row_start = pl.multiple_of(place // across * rows, 16)
    column_start = pl.multiple_of(place % across * columns, 128)
    return (pl.ds(row_start, rows), pl.ds(column_start, columns))


def split_kernel(places, across, held_ref, keep_ref, got_ref, rows_ref, held_out, *outs):
    place, _ = position()
    for k in range(places):
        out = outs[places - 1 - k]
        at = block_at(keep_ref, place ^ k, out.shape[0], out.shape[1], across)
        total = keep_ref[at] + got_ref[at].astype(F32)
        if k == 0:
            total = total + rows_ref[at].astype(F32)
        out[...] = total.astype(BF16)


def add_kernel(places, held_ref, *refs):
    total = refs[0][...].astype(F32)
    for k in range(1, places):
        total = total + refs[k][...].astype(F32)
    refs[places + 1][...] = total.astype(BF16)


def join_kernel(places, across, local, tick, held_ref, *refs):
    chunks, own_ref, out_ref, new_own_ref = (
        refs[:places], refs[places], refs[places + 2], refs[places + 3],
    )
    place, _ = position()
    for k in range(places):
        chunk = chunks[k]
        at = block_at(out_ref, place ^ k, chunk.shape[0], chunk.shape[1], across)
        out_ref[at] = chunk[...]

    active = lax.axis_index("section") == tick

    @pl.when(active)
    def _():
        new_own_ref[...] = packed(place, out_ref.shape[0], local, out_ref[...]).astype(BF16)

    @pl.when(jnp.logical_not(active))
    def _():
        new_own_ref[...] = own_ref[...]


def layer_kernel(tick, resident, half_rows, held_ref, mine_ref, other_ref, gain_ref, comb_ref, gate_ref,
                 up_ref, down_ref, held_out, keep_ref, send_ref, normed, part, gate_slots, down_slots,
                 gate_sems, down_sems, held_sem):
    experts = gate_ref.shape[1]
    hidden = gate_ref.shape[3]
    piece = hidden // 2
    rows = mine_ref.shape[0]

    active = lax.axis_index("section") == tick
    last_held = pltpu.make_async_copy(
        up_ref.at[0, resident - 1], held_out.at[2 * resident - 1], held_sem
    )
    if tick == 0:
        @pl.when(jnp.logical_not(active))
        def _():
            last_held.start()
            last_held.wait()

    @pl.when(active)
    def _():
        work = [(e, (0, 1)) for e in range(resident)]
        streamed = [(e, (s,)) for e in range(resident, experts) for s in range(2)]
        work = work[:-1] + streamed[:-1] + work[-1:] + streamed[-1:]
        queue = []
        for e, halves in work:
            for s in halves:
                if e >= resident:
                    queue += [("gate", e, s), ("up", e, s)]
                queue += [("down", e, s)]
        numbers, counts = {}, {"down": 0, "gate": 0}
        for kind, e, s in queue:
            pool = "down" if kind == "down" else "gate"
            numbers[kind, e, s] = (pool, counts[pool])
            counts[pool] += 1
        slots = {"down": DOWN_SLOTS, "gate": GATE_SLOTS}
        freed = {"down": 0, "gate": 0}
        pending = list(queue)

        def copy_of(item):
            kind, e, s = item
            pool, number = numbers[item]
            slot = number % slots[pool]
            cut = pl.ds(s * piece, piece)
            if kind == "down":
                return pltpu.make_async_copy(
                    down_ref.at[0, e, cut, :], down_slots.at[slot], down_sems.at[slot]
                ), down_slots.at[slot]
            source = gate_ref if kind == "gate" else up_ref
            return pltpu.make_async_copy(
                source.at[0, e, :, cut], gate_slots.at[slot], gate_sems.at[slot]
            ), gate_slots.at[slot]

        def issue():
            while pending:
                pool, number = numbers[pending[0]]
                if number >= freed[pool] + slots[pool]:
                    return
                copy_of(pending.pop(0))[0].start()

        def times(left, item):
            copy, ref = copy_of(item)
            copy.wait()
            result = jnp.dot(left, ref[...], preferred_element_type=F32)
            return result

        def done(item):
            freed[numbers[item][0]] += 1
            issue()

        issue()
        for ref, start in ((mine_ref, 0), (other_ref, half_rows)):
            values = ref[...].astype(F32)
            scale = lax.rsqrt(jnp.mean(values * values, axis=-1, keepdims=True) + 1e-05)
            normed[start:start + rows, :] = (values * scale * gain_ref[...]).astype(BF16)
            if half_rows > rows:
                normed[start + rows:start + half_rows, :] = jnp.zeros(
                    (half_rows - rows, values.shape[1]), BF16
                )

        def activated(gate, up, e):
            middle = 0.5 * gate
            return ((middle + middle * jnp.tanh(middle)) * up * comb_ref[:, e:e + 1]).astype(BF16)

        first = True
        for e, halves in work:
            if e < resident:
                gate = jnp.dot(normed[...], held_ref[e], preferred_element_type=F32)
                if tick == 0 and e == resident - 1:
                    last_held.wait()
                up = jnp.dot(normed[...], held_out[resident + e], preferred_element_type=F32)
                gated = activated(gate, up, e)
            for s in halves:
                if e < resident:
                    left = gated[:, s * piece:(s + 1) * piece]
                else:
                    gate = times(normed[...], ("gate", e, s))
                    done(("gate", e, s))
                    up = times(normed[...], ("up", e, s))
                    done(("up", e, s))
                    left = activated(gate, up, e)
                if first:
                    part[...] = times(left, ("down", e, s))
                else:
                    part[...] += times(left, ("down", e, s))
                if first and tick == 0:
                    last_held.start()
                first = False
                done(("down", e, s))
        keep_ref[...] = part[0:rows, :]
        send_ref[...] = part[half_rows:half_rows + rows, :].astype(BF16)


def split_rows_kernel(places, local, held_ref, keep_ref, got_ref, rows_ref, held_out, *outs):
    place, _ = position()
    rows = keep_ref.shape[0]
    total = (keep_ref[...] + got_ref[...].astype(F32)).astype(BF16)
    for k in range(1, places):
        outs[places - k][...] = packed(place ^ k, rows, local, total).astype(BF16)
    outs[0][...] = packed(place, rows, local, total) + packed(place, rows, local, rows_ref[...])


def last_kernel(places, *refs):
    own_ref, chunks, before_ref, out_ref = refs[0], refs[1:places], refs[places], refs[places + 1]
    total = own_ref[...]
    for chunk in chunks:
        total = total + chunk[...].astype(F32)
    last = lax.axis_index("section") == lax.axis_size("section") - 1
    result = jnp.where(last, total, before_ref[...].astype(F32))
    micro, local_rows, width = out_ref.shape
    for m in range(micro):
        for side in range(2):
            start = (side * micro + m) * local_rows
            columns = slice(side * width // 2, (side + 1) * width // 2)
            out_ref[m, :, columns] = result[start:start + local_rows, :].astype(BF16)


def on_device(inputs, gain, w_gate, w_up, w_down, routes, shares):
    sections = lax.axis_size("section")
    places = lax.axis_size("fsdp") // 2
    micro, local_rows, width = inputs.shape
    _, experts, _, hidden = w_gate.shape
    local = micro * local_rows
    rows = places * local
    half_rows = round_up(rows, 64)
    across = places
    while (width // across) % 128 or width % across:
        across //= 2
    block = (rows // (places // across), width // across)
    resident = min(experts, RESIDENT_BYTES // (4 * width * hidden))

    chosen = routes[0][:, None] == jnp.arange(experts, dtype=jnp.int32)[None, :, None, None]
    comb = jnp.sum(jnp.where(chosen, shares[0][:, None], 0.0), axis=3)

    def swapped(array):
        return moved(array, sections, places, lambda s, p, c: (s, p, 1 - c))

    def within(array, k):
        return moved(array, sections, places, lambda s, p, c: (s, p ^ k, c))

    def full(leg, k):
        return k == places - 1 if leg == 0 else k < 2

    def onward(array, tick, k, leg):
        def target(section, place, half):
            if not full(leg, k) and section != ring_of(tick, sections, half)[leg]:
                return None
            return (after(tick, sections, half, section), place ^ k, half)

        return moved(array, sections, places, target)

    def like(shape, dtype=BF16):
        return jax.ShapeDtypeStruct(shape, dtype)

    pieces = [inputs] + [within(inputs, k) for k in range(1, places)]
    held, comb = hold(w_gate, w_up, comb, resident, rows, half_rows, local_rows)
    slot = (2 * local, width // 2)
    held, mine, own = chained(
        functools.partial(entry_kernel, places),
        [like((rows, width)), like(slot)], pieces, held,
    )
    stream_flops = 6 * 2 * half_rows * width * hidden * experts
    stream_bytes = 2 * 3 * width * hidden * experts - 4 * width * hidden * resident
    for tick in range(sections):
        other = swapped(mine)
        held, keep, send = chained(
            functools.partial(layer_kernel, tick, resident, half_rows),
            [like((rows, width), F32), like((rows, width))],
            [mine, other, gain, comb, w_gate, w_up, w_down],
            held,
            specs=[VMEM, VMEM, VMEM, VMEM, HBM, HBM, HBM],
            scratch=[
                pltpu.VMEM((2 * half_rows, width), BF16),
                pltpu.VMEM((2 * half_rows, width), F32),
                pltpu.VMEM((GATE_SLOTS, width, hidden // 2), BF16),
                pltpu.VMEM((DOWN_SLOTS, hidden // 2, width), BF16),
                pltpu.SemaphoreType.DMA((GATE_SLOTS,)),
                pltpu.SemaphoreType.DMA((DOWN_SLOTS,)),
                pltpu.SemaphoreType.DMA,
            ],
            pinned=2,
            flops=stream_flops,
            moved_bytes=stream_bytes,
        )
        got = swapped(send)
        if tick + 1 == sections:
            break
        held, *blocks = chained(
            functools.partial(split_kernel, places, across),
            [like(block)] * places, [keep, got, mine], held,
        )
        blocks = [onward(blocks[places - 1 - k], tick, k, 0) for k in reversed(range(places))]
        held, summed = chained(
            functools.partial(add_kernel, places), [like(block)], blocks, held
        )
        blocks = [onward(summed, tick, k, 1) for k in reversed(range(places))][::-1]
        held, mine, own = chained(
            functools.partial(join_kernel, places, across, local, tick + 1),
            [like((rows, width)), like(slot)], blocks + [own], held,
        )
    before = moved(own, sections, places, lambda s, p, c: ((s - 1) % sections, p, c))
    held, *pieces = chained(
        functools.partial(split_rows_kernel, places, local),
        [like(slot, F32)] + [like(slot)] * (places - 1),
        [keep, got, mine], held,
    )
    pieces = [pieces[0]] + [within(pieces[places - k], k) for k in reversed(range(1, places))]
    result = pl.pallas_call(
        functools.partial(last_kernel, places),
        out_shape=like((micro, local_rows, width)),
        in_specs=[VMEM] * (places + 1),
        out_specs=VMEM,
    )(*[pltpu.with_memory_space_constraint(array, pltpu.VMEM) for array in (*pieces, before)])
    return result[None]


def solution(mesh):
    placed = (
        P(None, "fsdp", None),
        P("section", None),
        P("section", None, None, "fsdp"),
        P("section", None, None, "fsdp"),
        P("section", None, "fsdp", None),
        P("section", None, None, None),
        P("section", None, None, None),
    )
    return jax.shard_map(
        on_device,
        mesh=mesh,
        in_specs=placed,
        out_specs=P("section", None, "fsdp", None),
        check_vma=False,
    )
```
